128 devices in a mesh: space: 16 (over y, x_hi, core), member: 8 (over z, x_lo).
Axes of the slice: x: 4 (x_hi: 2, x_lo: 2; x = x_hi * 2 + x_lo), y: 4, z: 4, core: 2. Of those that a mesh axis runs over, the one named last changes fastest.
Arguments:
- temp_start: float32 [16, 10, 640, 640], P('member', None, 'space'), may hold values from -6 to 6
- cotangent: float32 [16, 10, 640, 640], P('member', None, 'space'), may hold values from -6 to 6
- forcing: float32 [16, 640, 640], P('member', 'space'), may hold values from -2 to 2
- soil_class: int32 [640, 640], P('space'), may hold values from 0 to 11
- conductivity: float32 [12, 10], replicated, may hold values from 0.03 to 0.18
- parent_field: float32 [10, 32, 32], P(None, 'space'), may hold values from -6 to 6
- tile_map: int32 [16], replicated, may hold values from 0 to 15, as said below
Outputs:
- temp_final: float32 [16, 10, 640, 640], P('member', None, 'space')
- adjoint_start: float32 [16, 10, 640, 640], P('member', None, 'space')
- parent_grad: float32 [10, 32, 32], P(None, 'space')
The draws below stay inside these ranges and needn't reach their ends.
Inputs may be any that keep to these rules, and one draw needn't show every extreme that they name: `tile_map`: each parent tile holds exactly one nest tile.
All inputs are finite; a program needn't handle non-finite values.
Results may differ from the reference program's by a relative error of at most 0.00013.
Values sent between devices are 32-bit elements; how exact they have to be, the bound alone decides.
No kernel may reach another device: no remote copies, remote signals or barrier semaphores. Data moves between devices by JAX's collectives and lax.ppermute only.
A program may use at most 128 MiB of HBM per device.

```python
import math
import jax
import jax.numpy as jnp

LAYERS = 10
CLASSES = 12
R = 20
TX = 40
TY = 640
ITERS = 4
MEMBERS = 16
NX = 640
NPX = 32
PY = 32
N_SPACE = 16


def draw_tile_map(key, part):
    key = jax.random.fold_in(key, 17)
    places = jnp.arange(N_SPACE, dtype=jnp.int32)
    return jax.random.permutation(key, places).astype(jnp.int32)


def with_ends(drawn, own_key, low, largest):
    longest = drawn.shape.index(max(drawn.shape))
    spots = []
    for shift in (0, 1):
        where = [jax.random.randint(jax.random.fold_in(own_key, axis), (), 0, length) for axis, length in enumerate(drawn.shape)]
        where[longest] = (where[longest] + shift) % drawn.shape[longest]
        spots.append(tuple(where))
    return drawn.at[spots[0]].set(low).at[spots[1]].set(largest)


def block_levels(key, dims, pieces, low, high):
    def one(position, blocks):
        steps = jax.random.uniform(jax.random.fold_in(jax.random.fold_in(key, 6), position), (blocks,), jnp.float32, low / len(pieces), high / len(pieces))
        return jnp.repeat(jnp.exp(steps), dims[position] // blocks).reshape((-1,) + (1,) * (len(dims) - position - 1))

    gain = one(*pieces[0])
    for cut in pieces[1:]:
        gain = gain * one(*cut)
    return gain


def scatter_about(key, shape, spread, bound, split=(), kind=jnp.bfloat16):
    gain = block_levels(key, shape, split, -0.22, 0.18) if split else 1.0
    result = jax.random.normal(key, shape, jnp.float32) * spread * gain
    return jnp.minimum(jnp.maximum(result, -bound), bound).astype(kind)


def setup_inputs(seed: int = 0) -> dict:
    key_of = jax.random.split(jax.random.key(seed), 8)
    return {
        "temp_start": scatter_about(key_of[0], (MEMBERS, LAYERS, NX, TY), 1.0, 6.0, ((0, 8), (2, 16)), jnp.float32),
        "cotangent": scatter_about(key_of[1], (MEMBERS, LAYERS, NX, TY), 1.0, 6.0, ((0, 8), (2, 16)), jnp.float32),
        "forcing": scatter_about(key_of[2], (MEMBERS, NX, TY), 0.3, 2.0, ((0, 8), (1, 16)), jnp.float32),
        "soil_class": with_ends(jax.random.randint(key_of[3], (NX, TY), 0, CLASSES), jax.random.fold_in(key_of[3], 1), 0, CLASSES - 1).astype(jnp.int32),
        "conductivity": jnp.clip(jnp.exp(jax.random.uniform(key_of[4], (CLASSES, LAYERS), jnp.float32, math.log(0.03), math.log(0.18))), 0.03, 0.18),
        "parent_field": scatter_about(key_of[5], (LAYERS, NPX, PY), 1.0, 6.0, ((1, 16),), jnp.float32),
        "tile_map": draw_tile_map(jax.random.fold_in(key_of[7], 71), 0),
    }


relax_rate = 0.1
vertical_rate = 0.05


def vertical_term(field):
    above_layer = jnp.concatenate([field[:, :1], field[:, :-1]], 1)
    below_layer = jnp.concatenate([field[:, 1:], field[:, -1:]], 1)
    return above_layer + below_layer - 2.0 * field


def planar_term(field):
    padded = jnp.pad(field, ((0, 0), (0, 0), (1, 1), (1, 1)))
    total = padded[:, :, 2:, 1:-1] + padded[:, :, :-2, 1:-1]
    total = total + padded[:, :, 1:-1, 2:] + padded[:, :, 1:-1, :-2]
    return total - 4.0 * field


def reference(temp_start, cotangent, forcing, soil_class, conductivity, parent_field, tile_map):
    kappa = jnp.transpose(conductivity[soil_class], (2, 0, 1))
    rows_per = TX // R
    row_index = (tile_map[:, None] * rows_per + jnp.arange(rows_per, dtype=jnp.int32)[None, :]).reshape(-1).astype(jnp.int32)
    arranged = parent_field[:, row_index, :]
    target = jnp.repeat(jnp.repeat(arranged, R, axis=1), R, axis=2)
    layer_top = (jnp.arange(LAYERS) == 0)[None, :, None, None]
    temp = temp_start
    for section in range(ITERS):
        updated = temp + kappa * planar_term(temp) + vertical_rate * vertical_term(temp) + relax_rate * (target - temp)
        temp = updated + jnp.where(layer_top, forcing[:, None], jnp.zeros((), jnp.float32))
    adjoint = cotangent
    running = cotangent
    for section in range(ITERS):
        adjoint = adjoint + planar_term(kappa * adjoint) + vertical_rate * vertical_term(adjoint) - relax_rate * adjoint
        if section < ITERS - 1:
            running = running + adjoint
    summed = jnp.sum(running, 0)
    blocks = summed.reshape(LAYERS, NX // R, R, TY // R, R).sum(axis=(2, 4)) * (relax_rate / (R * R))
    parent_grad = jnp.zeros_like(parent_field).at[:, row_index, :].set(blocks)
    return temp, adjoint, parent_grad
```

```python
import functools

import jax
import jax.numpy as jnp
from jax import lax
from jax.experimental import pallas as pl
from jax.experimental.pallas import tpu as pltpu
from jax.sharding import PartitionSpec as P

R = 20
ITERS = 4
HALO = ITERS
LANES = 128
RELAX = 0.1
VERT = 0.05
KEEP = 1.0 - RELAX - 2.0 * VERT
f32 = jnp.float32
HIGHEST = lax.Precision.HIGHEST

VM = pl.BlockSpec(memory_space=pltpu.VMEM)
SM = pl.BlockSpec(memory_space=pltpu.SMEM)
HB = pl.BlockSpec(memory_space=pl.ANY)
PARAMS = pltpu.CompilerParams(vmem_limit_bytes=56 * 1024 * 1024)


def cols_of(c):
    return slice(c * LANES, (c + 1) * LANES)


def spread(group, rows, width):
    y = lax.broadcasted_iota(jnp.int32, (width, LANES), 0)
    lane = lax.broadcasted_iota(jnp.int32, (width, LANES), 1)
    return (y // rows + 32 * group == lane).astype(f32)


def pack_kernel(cot, temp, forcing, soil, parent, a_cot, b_cot, a_temp, b_temp, tiles, edge_c, edge_t, edge_f, edge_s, flat, sems):
    rows = cot.shape[2]
    odd = lax.axis_index("space") % 2
    copies = []
    for side, start in ((0, 0), (1, rows - 8)):
        cut = pl.ds(start, 8)
        copies.append(pltpu.make_async_copy(cot.at[:, :, cut, :], edge_c.at[side], sems.at[side, 0]))
        copies.append(pltpu.make_async_copy(soil.at[cut, :], edge_s.at[side], sems.at[side, 1]))
        copies.append(pltpu.make_async_copy(temp.at[:, :, cut, :], edge_t.at[side], sems.at[side, 2]))
        copies.append(pltpu.make_async_copy(forcing.at[:, cut, :], edge_f.at[side], sems.at[side, 3]))
    for copy in copies:
        copy.start()
    members, layers = cot.shape[:2]
    groups = -(-2 * layers // 8)
    flat[...] = jnp.zeros_like(flat)
    for l in range(layers):
        flat[2 * l:2 * l + 2, :] = parent[l]
    packed = jnp.zeros((8, LANES), f32)
    for g in range(groups):
        packed = packed + jnp.dot(flat[8 * g:8 * g + 8, :], spread(g, 1, flat.shape[1]), precision=HIGHEST)
    for i in range(tiles.shape[0]):
        tiles[i] = packed
    for copy in copies:
        copy.wait()
    for parity in (0, 1):
        @pl.when(odd == parity)
        def _():
            low, high = (slice(0, 4), slice(4, 8))
            for side, cut in ((0, low), (1, high)):
                to_a = (side == 1) == (parity == 0)
                oc, ot = (a_cot, a_temp) if to_a else (b_cot, b_temp)
                for m in range(members):
                    for l in range(layers):
                        oc[m * layers + l] = edge_c[side, m, l, cut, :]
                        ot[m * layers + l] = edge_t[side, m, l, cut, :]
                    ot[members * layers + m] = edge_f[side, m, cut, :]
                oc[members * layers] = edge_s[side, cut, :].astype(f32) + 1.0


def side_rows(odd, a_ref, b_ref, p):
    a, b = a_ref[p], b_ref[p]
    return jnp.where(odd == 1, a, b), jnp.where(odd == 1, b, a)


def fill_kappa(soil, a_cot, b_cot, cond, odd, layers, S, K, C):
    rows, cols = soil.shape
    top, bottom = side_rows(odd, a_cot, b_cot, a_cot.shape[0] - 1)
    lane = lax.broadcasted_iota(jnp.int32, (8, LANES), 1)
    for c in range(cols // LANES):
        S[c, 0:HALO, :] = top[:, cols_of(c)].astype(jnp.int32) - 1
        S[c, rows + HALO:, :] = bottom[:, cols_of(c)].astype(jnp.int32) - 1
        S[c, HALO:rows + HALO, :] = soil[:, cols_of(c)]
    classes = cond.shape[0]
    for l in range(layers):
        table = jnp.zeros((8, LANES), f32)
        for k in range(classes):
            table = jnp.where(lane == k, cond[k, l], table)
        for c in range(cols // LANES):
            for i in range((rows + 2 * HALO) // 8):
                cut = slice(8 * i, 8 * i + 8)
                idx = S[c, cut, :]
                idx = jnp.where(idx < 0, LANES - 1, idx)
                kappa = jnp.take_along_axis(table, idx, axis=1)
                K[l, c, cut, :] = kappa
                C[l, c, cut, :] = KEEP - 4.0 * kappa


def fill_field(field, a_ref, b_ref, odd, X):
    members, layers, rows, cols = field.shape

    def plane(p, carry):
        top, bottom = side_rows(odd, a_ref, b_ref, p)
        for c in range(cols // LANES):
            X[0, p, c, 0:HALO, :] = top[:, cols_of(c)]
            X[0, p, c, rows + HALO:, :] = bottom[:, cols_of(c)]
            X[0, p, c, HALO:rows + HALO, :] = field[p // layers, p % layers, :, cols_of(c)]
        return carry

    lax.fori_loop(0, members * layers, plane, 0)


def sideways(center):
    lane = lax.broadcasted_iota(jnp.int32, (8, LANES), 1)
    count = len(center)
    right = [pltpu.roll(v, 1, 1) for v in center]
    left = [pltpu.roll(v, LANES - 1, 1) for v in center]
    out = []
    for c in range(count):
        before = right[c - 1] if c > 0 else jnp.zeros((8, LANES), f32)
        after = left[c + 1] if c < count - 1 else jnp.zeros((8, LANES), f32)
        out.append(jnp.where(lane == 0, before, right[c]) + jnp.where(lane == LANES - 1, after, left[c]))
    return out


def chunk_start(i, rows):
    return jnp.minimum(1 + 8 * i, rows + 2 * HALO - 9)


def adjoint_kernel(cot, a_cot, b_cot, soil, cond, tile_map, adj, blocks, X, W, K, C, S, RS, BS):
    members, layers, rows, cols = cot.shape
    position = lax.axis_index("space")
    odd = position % 2
    nb = cols // LANES
    chunks = RS.shape[0]
    fill_kappa(soil, a_cot, b_cot, cond, odd, layers, S, K, C)
    fill_field(cot, a_cot, b_cot, odd, X)

    def weigh(p, carry):
        for c in range(nb):
            W[0, p, c] = X[0, p, c] * K[p % layers, c]
        return carry

    lax.fori_loop(0, members * layers, weigh, 0)

    for k in range(ITERS):
        src, dst = k % 2, 1 - k % 2
        last = k == ITERS - 1

        def chunk(i, carry):
            r = HALO + 8 * i if last else chunk_start(i, rows)
            mid, up, down = pl.ds(r, 8), pl.ds(r - 1, 8), pl.ds(r + 1, 8)
            above = [[X[src, m * layers, c, mid, :] for c in range(nb)] for m in range(members)]
            here = above
            for l in range(layers):
                total = [None] * nb
                after = []
                for m in range(members):
                    p = m * layers + l
                    below = [X[src, p + 1, c, mid, :] for c in range(nb)] if l < layers - 1 else here[m]
                    after.append(below)
                    side = sideways([W[src, p, c, mid, :] for c in range(nb)])
                    for c in range(nb):
                        planar = side[c] + (W[src, p, c, up, :] + W[src, p, c, down, :])
                        new = C[l, c, mid, :] * here[m][c] + planar + VERT * (above[m][c] + below[c])
                        if l == 0 or l == layers - 1:
                            pass
                        if last:
                            adj[m, l, pl.ds(pl.multiple_of(8 * i, 8), 8), cols_of(c)] = new
                        else:
                            X[dst, p, c, mid, :] = new
                            W[dst, p, c, mid, :] = K[l, c, mid, :] * new
                            part = new + here[m][c] if k == 0 else new
                            total[c] = part if total[c] is None else total[c] + part
                if not last:
                    for c in range(nb):
                        RS[i, l, c] = total[c] if k == 0 else RS[i, l, c] + total[c]
                above, here = here, after
            return carry

        lax.fori_loop(0, rows // 8 if last else chunks, chunk, 0)
        if k == ITERS - 2:
            row = lax.broadcasted_iota(jnp.int32, (8, LANES), 0)
            BS[...] = jnp.zeros_like(BS)
            for l in range(layers):
                for c in range(nb):
                    sums = [jnp.zeros((8, LANES), f32)] * 2
                    done = HALO
                    for i in range(chunks):
                        start = min(1 + 8 * i, rows + 2 * HALO - 9)
                        value = RS[i, l, c]
                        for b in range(2):
                            lo = max(done, HALO + R * b) - start
                            hi = min(start + 8, HALO + R * (b + 1)) - start
                            if hi <= max(lo, 0):
                                continue
                            part = value if lo <= 0 and hi >= 8 else jnp.where((row >= lo) & (row < hi), value, 0.0)
                            sums[b] = sums[b] + part
                        done = start + 8
                    for b in range(2):
                        BS[2 * l + b:2 * l + b + 1, cols_of(c)] = jnp.sum(sums[b], axis=0, keepdims=True)
            packed = jnp.zeros((8, LANES), f32)
            for g in range(BS.shape[0] // 8):
                packed = packed + jnp.dot(BS[8 * g:8 * g + 8, :], spread(g, R, cols), precision=HIGHEST)
            packed = packed * (RELAX / (R * R))
            blocks[...] = jnp.zeros_like(blocks)
            spaces = tile_map.shape[0]
            owner = tile_map[position]
            for m in range(blocks.shape[0] // spaces):
                blocks[m * spaces + owner] = packed


def forward_kernel(temp, forcing, a_temp, b_temp, a_cot, b_cot, soil, cond, tiles, tile_map, out, X, K, C, S, T, F, TE):
    members, layers, rows, cols = temp.shape
    spaces = tile_map.shape[0]
    position = lax.axis_index("space")
    odd = position % 2
    nb = cols // LANES
    ext = rows + 2 * HALO
    fill_kappa(soil, a_cot, b_cot, cond, odd, layers, S, K, C)
    fill_field(temp, a_temp, b_temp, odd, X)
    around = []
    for shift in (-1, 0, 1):
        where = jnp.minimum(jnp.maximum(position + shift, 0), spaces - 1)
        inside = jnp.logical_and(position + shift >= 0, position + shift < spaces)
        around.append(jnp.where(inside, tiles[tile_map[where]], 0.0))
    stack = jnp.concatenate(around, axis=0) * RELAX
    for g in range(TE.shape[0]):
        lane = lax.broadcasted_iota(jnp.int32, (LANES, cols), 0)
        y = lax.broadcasted_iota(jnp.int32, (LANES, cols), 1)
        TE[g] = jnp.dot(stack, (y // R + 32 * g == lane).astype(f32), precision=HIGHEST)

    def levels(l, t, b):
        n = 2 * l + b
        return TE[n // 8, 8 * t + n % 8:8 * t + n % 8 + 1, :]

    for l in range(layers):
        bands = [(0, HALO, levels(l, 0, 1)), (HALO, HALO + R, levels(l, 1, 0)), (HALO + R, HALO + 2 * R, levels(l, 1, 1)), (HALO + 2 * R, ext, levels(l, 2, 0))]
        for c in range(nb):
            for lo, hi, value in bands:
                T[l, c, lo:hi, :] = jnp.broadcast_to(value[:, cols_of(c)], (hi - lo, LANES))
    for m in range(members):
        top, bottom = side_rows(odd, a_temp, b_temp, members * layers + m)
        for c in range(nb):
            F[m, c, 0:HALO, :] = T[0, c, 0:HALO, :] + top[:, cols_of(c)]
            F[m, c, rows + HALO:, :] = T[0, c, rows + HALO:, :] + bottom[:, cols_of(c)]
            F[m, c, HALO:rows + HALO, :] = T[0, c, HALO:rows + HALO, :] + forcing[m, :, cols_of(c)]

    for k in range(ITERS):
        src, dst = k % 2, 1 - k % 2
        last = k == ITERS - 1

        def chunk(i, carry):
            r = HALO + 8 * i if last else chunk_start(i, rows)
            mid, up, down = pl.ds(r, 8), pl.ds(r - 1, 8), pl.ds(r + 1, 8)
            above = [[X[src, m * layers, c, mid, :] for c in range(nb)] for m in range(members)]
            here = above
            for l in range(layers):
                after = []
                for m in range(members):
                    p = m * layers + l
                    below = [X[src, p + 1, c, mid, :] for c in range(nb)] if l < layers - 1 else here[m]
                    after.append(below)
                    side = sideways(here[m])
                    for c in range(nb):
                        around = side[c] + (X[src, p, c, up, :] + X[src, p, c, down, :])
                        source = F[m, c, mid, :] if l == 0 else T[l, c, mid, :]
                        new = C[l, c, mid, :] * here[m][c] + K[l, c, mid, :] * around + (VERT * (above[m][c] + below[c]) + source)
                        if last:
                            out[m, l, pl.ds(pl.multiple_of(8 * i, 8), 8), cols_of(c)] = new
                        else:
                            X[dst, p, c, mid, :] = new
                above, here = here, after
            return carry

        lax.fori_loop(0, rows // 8 if last else -(-(ext - 2) // 8), chunk, 0)


def sum_kernel(received, out, total):
    value = received[0]
    for i in range(1, received.shape[0]):
        value = value + received[i]
    total[...] = value
    layers, per, width = out.shape
    for l in range(layers):
        for b in range(per):
            n = per * l + b
            out[l, b:b + 1, :] = total[n % 8:n % 8 + 1, 32 * (n // 8):32 * (n // 8) + width]


def body(temp_start, cotangent, forcing, soil_class, conductivity, parent_field, tile_map):
    members, layers, rows, cols = temp_start.shape
    nb = cols // LANES
    spaces = lax.axis_size("space")
    groups = lax.axis_size("member")
    planes = members * layers
    ext = rows + 2 * HALO
    chunks = -(-(ext - 2) // 8)
    pieces = -(-2 * layers // 8)
    shape = lambda *dims: jax.ShapeDtypeStruct(dims, f32)
    a_cot, b_cot, a_temp, b_temp, tiles = pl.pallas_call(
        pack_kernel,
        out_shape=(shape(planes + 1, HALO, cols), shape(planes + 1, HALO, cols), shape(planes + members, HALO, cols), shape(planes + members, HALO, cols), shape(spaces, 8, LANES)),
        in_specs=[HB, HB, HB, HB, VM],
        out_specs=[VM] * 5,
        scratch_shapes=[
            pltpu.VMEM((2, members, layers, 8, cols), f32),
            pltpu.VMEM((2, members, layers, 8, cols), f32),
            pltpu.VMEM((2, members, 8, cols), f32),
            pltpu.VMEM((2, 8, cols), jnp.int32),
            pltpu.VMEM((8 * pieces, parent_field.shape[2]), f32),
            pltpu.SemaphoreType.DMA((2, 4)),
        ],
        compiler_params=PARAMS,
        name="pack",
    )(cotangent, temp_start, forcing, soil_class, parent_field)
    pair = [(i, i ^ 1) for i in range(spaces)]
    across = [(i, i + 1) for i in range(1, spaces - 1, 2)] + [(i + 1, i) for i in range(1, spaces - 1, 2)]
    a_cot = lax.ppermute(a_cot, "space", pair)
    b_cot = lax.ppermute(b_cot, "space", across)
    a_temp = lax.ppermute(a_temp, "space", pair)
    b_temp = lax.ppermute(b_temp, "space", across)
    tiles = lax.all_to_all(tiles, "space", 0, 0, tiled=True)
    flops = 15 * planes * ext * cols * ITERS
    cost = pl.CostEstimate(flops=flops, bytes_accessed=4 * 2 * planes * rows * cols, transcendentals=0)
    adjoint, blocks = pl.pallas_call(
        adjoint_kernel,
        out_shape=(jax.ShapeDtypeStruct(cotangent.shape, f32), shape(groups * spaces, 8, LANES)),
        in_specs=[VM, VM, VM, VM, SM, SM],
        out_specs=[VM, VM],
        scratch_shapes=[
            pltpu.VMEM((2, planes, nb, ext, LANES), f32),
            pltpu.VMEM((2, planes, nb, ext, LANES), f32),
            pltpu.VMEM((layers, nb, ext, LANES), f32),
            pltpu.VMEM((layers, nb, ext, LANES), f32),
            pltpu.VMEM((nb, ext, LANES), jnp.int32),
            pltpu.VMEM((chunks, layers, nb, 8, LANES), f32),
            pltpu.VMEM((8 * pieces, cols), f32),
        ],
        compiler_params=PARAMS,
        cost_estimate=cost,
        name="adjoint",
    )(cotangent, a_cot, b_cot, soil_class, conductivity, tile_map)
    received = lax.all_to_all(blocks, ("member", "space"), 0, 0, tiled=True)
    temp = pl.pallas_call(
        forward_kernel,
        out_shape=jax.ShapeDtypeStruct(temp_start.shape, f32),
        in_specs=[VM, VM, VM, VM, VM, VM, VM, SM, VM, SM],
        out_specs=VM,
        scratch_shapes=[
            pltpu.VMEM((2, planes, nb, ext, LANES), f32),
            pltpu.VMEM((layers, nb, ext, LANES), f32),
            pltpu.VMEM((layers, nb, ext, LANES), f32),
            pltpu.VMEM((nb, ext, LANES), jnp.int32),
            pltpu.VMEM((layers, nb, ext, LANES), f32),
            pltpu.VMEM((members, nb, ext, LANES), f32),
            pltpu.VMEM((pieces, 24, cols), f32),
        ],
        compiler_params=PARAMS,
        cost_estimate=cost,
        name="forward",
    )(temp_start, forcing, a_temp, b_temp, a_cot, b_cot, soil_class, conductivity, tiles, tile_map)
    parent_grad = pl.pallas_call(
        sum_kernel,
        out_shape=shape(*parent_field.shape),
        in_specs=[VM],
        out_specs=VM,
        scratch_shapes=[pltpu.VMEM((8, LANES), f32)],
        compiler_params=PARAMS,
        name="collect",
    )(received)
    return temp, adjoint, parent_grad


def solution(mesh):
    return jax.shard_map(
        body,
        mesh=mesh,
        in_specs=(
            P("member", None, "space", None),
            P("member", None, "space", None),
            P("member", "space", None),
            P("space", None),
            P(),
            P(None, "space", None),
            P(),
        ),
        out_specs=(
            P("member", None, "space", None),
            P("member", None, "space", None),
            P(None, "space", None),
        ),
        check_vma=False,
    )
```

```python
import functools

import jax
import jax.numpy as jnp
from jax import lax
from jax.experimental import pallas as pl
from jax.experimental.pallas import tpu as pltpu
from jax.sharding import PartitionSpec as P

R = 20
ITERS = 4
HALO = ITERS
LANES = 128
RELAX = 0.1
VERT = 0.05
KEEP = 1.0 - RELAX - 2.0 * VERT
f32 = jnp.float32
HIGHEST = lax.Precision.HIGHEST

VM = pl.BlockSpec(memory_space=pltpu.VMEM)
SM = pl.BlockSpec(memory_space=pltpu.SMEM)
HB = pl.BlockSpec(memory_space=pl.ANY)
SMALL = pltpu.CompilerParams(vmem_limit_bytes=6 * 1024 * 1024)
PARAMS = pltpu.CompilerParams(vmem_limit_bytes=24 * 1024 * 1024)


def far(x):
    return pltpu.with_memory_space_constraint(x, pltpu.HBM)


def near(x):
    return pltpu.with_memory_space_constraint(x, pltpu.VMEM)


def cols_of(c):
    return slice(c * LANES, (c + 1) * LANES)


def spread(group, rows, width):
    y = lax.broadcasted_iota(jnp.int32, (width, LANES), 0)
    lane = lax.broadcasted_iota(jnp.int32, (width, LANES), 1)
    return (y // rows + 32 * group == lane).astype(f32)


def send_rows(odd, pieces):
    for parity in (0, 1):
        @pl.when(odd == parity)
        def _():
            for take, plane, near_msg, far_msg in pieces:
                low, high = take(True), take(False)
                first, second = (far_msg, near_msg) if parity == 0 else (near_msg, far_msg)
                first[plane] = low()
                second[plane] = high()


def taker(ref, *index, convert=None):
    def take(top):
        def get():
            value = ref[(0 if top else 1, *index, slice(0, HALO) if top else slice(8 - HALO, 8), slice(None))]
            return convert(value) if convert else value

        return get

    return take


def edge_copies(pairs, rows, sems):
    out = []
    for n, (field, edges) in enumerate(pairs):
        for side, start in ((0, 0), (1, rows - 8)):
            cut = (*[slice(None)] * (len(field.shape) - 2), pl.ds(start, 8), slice(None))
            out.append(pltpu.make_async_copy(field.at[cut], edges.at[side], sems.at[n, side]))
    return out


def pack_kernel(cot, temp, forcing, soil, parent, a_msg, b_msg, tiles, flat, edge_c, edge_t, edge_f, edge_s, held, sems, sem):
    members, layers, rows = cot.shape[:3]
    get_parent = pltpu.make_async_copy(parent, held, sem)
    get_parent.start()
    copies = edge_copies(((cot, edge_c), (temp, edge_t), (forcing, edge_f), (soil, edge_s)), rows, sems)
    for copy in copies:
        copy.start()
    odd = lax.axis_index("space") % 2
    flat[...] = jnp.zeros_like(flat)
    get_parent.wait()
    for l in range(layers):
        flat[2 * l:2 * l + 2, :] = held[l]
    packed = jnp.zeros((8, LANES), f32)
    for g in range(flat.shape[0] // 8):
        packed = packed + jnp.dot(flat[8 * g:8 * g + 8, :], spread(g, 1, flat.shape[1]), precision=HIGHEST)
    for i in range(tiles.shape[0]):
        tiles[i] = packed
    for copy in copies:
        copy.wait()
    planes = members * layers
    pieces = []
    for m in range(members):
        for l in range(layers):
            pieces.append((taker(edge_c, m, l), m * layers + l, a_msg, b_msg))
            pieces.append((taker(edge_t, m, l), planes + m * layers + l, a_msg, b_msg))
        pieces.append((taker(edge_f, m), 2 * planes + m, a_msg, b_msg))
    pieces.append((taker(edge_s, convert=lambda v: v.astype(f32) + 1.0), 2 * planes + members, a_msg, b_msg))
    send_rows(odd, pieces)


def side_rows(odd, a_ref, b_ref, p):
    a, b = a_ref[p], b_ref[p]
    return jnp.where(odd == 1, a, b), jnp.where(odd == 1, b, a)


def fill_kappa(soil, a_msg, b_msg, cond, odd, layers, S, K, C):
    rows, cols = soil.shape
    top, bottom = side_rows(odd, a_msg, b_msg, a_msg.shape[0] - 1)
    lane = lax.broadcasted_iota(jnp.int32, (8, LANES), 1)
    for c in range(cols // LANES):
        S[c, 0:HALO, :] = top[:, cols_of(c)].astype(jnp.int32) - 1
        S[c, rows + HALO:, :] = bottom[:, cols_of(c)].astype(jnp.int32) - 1
        S[c, HALO:rows + HALO, :] = soil[:, cols_of(c)]
    classes = cond.shape[0]
    for l in range(layers):
        table = jnp.zeros((8, LANES), f32)
        for k in range(classes):
            table = jnp.where(lane == k, cond[k, l], table)
        for c in range(cols // LANES):
            for i in range((rows + 2 * HALO) // 8):
                cut = slice(8 * i, 8 * i + 8)
                idx = S[c, cut, :]
                idx = jnp.where(idx < 0, LANES - 1, idx)
                kappa = jnp.take_along_axis(table, idx, axis=1)
                K[l, c, cut, :] = kappa
                C[l, c, cut, :] = KEEP - 4.0 * kappa


def fill_field(field, a_ref, b_ref, odd, X, first):
    members, layers, rows, cols = field.shape

    def plane(p, carry):
        top, bottom = side_rows(odd, a_ref, b_ref, first + p)
        for c in range(cols // LANES):
            X[0, p, c, 0:HALO, :] = top[:, cols_of(c)]
            X[0, p, c, rows + HALO:, :] = bottom[:, cols_of(c)]
            X[0, p, c, HALO:rows + HALO, :] = field[p // layers, p % layers, :, cols_of(c)]
        return carry

    lax.fori_loop(0, members * layers, plane, 0)


def sideways(center):
    lane = lax.broadcasted_iota(jnp.int32, (8, LANES), 1)
    count = len(center)
    right = [pltpu.roll(v, 1, 1) for v in center]
    left = [pltpu.roll(v, LANES - 1, 1) for v in center]
    out = []
    for c in range(count):
        before = right[c - 1] if c > 0 else jnp.zeros((8, LANES), f32)
        after = left[c + 1] if c < count - 1 else jnp.zeros((8, LANES), f32)
        out.append(jnp.where(lane == 0, before, right[c]) + jnp.where(lane == LANES - 1, after, left[c]))
    return out


def chunk_start(i, rows):
    return jnp.minimum(1 + 8 * i, rows + 2 * HALO - 9)


def row_copy(src, dst, sems, i):
    cut = pl.ds(pl.multiple_of(8 * i, 8), 8)
    return pltpu.make_async_copy(src.at[:, :, cut, :], dst.at[:, :, cut, :], sems.at[i])


def adjoint_kernel(cot, a_msg, b_msg, soil, cond, tile_map, adj_out, blocks_out, X, W, K, C, S, RS, BS, blocks, adj, sems, sem):
    members, layers, rows, cols = cot.shape
    position = lax.axis_index("space")
    odd = position % 2
    nb = cols // LANES
    chunks = RS.shape[0]
    send_blocks = pltpu.make_async_copy(blocks, blocks_out, sem.at[0])
    fill_kappa(soil, a_msg, b_msg, cond, odd, layers, S, K, C)
    fill_field(cot, a_msg, b_msg, odd, X, 0)

    def weigh(p, carry):
        for c in range(nb):
            W[0, p, c] = X[0, p, c] * K[p % layers, c]
        return carry

    lax.fori_loop(0, members * layers, weigh, 0)

    for k in range(ITERS):
        src, dst = k % 2, 1 - k % 2
        last = k == ITERS - 1

        def chunk(i, carry):
            r = HALO + 8 * i if last else chunk_start(i, rows)
            mid, up, down = pl.ds(r, 8), pl.ds(r - 1, 8), pl.ds(r + 1, 8)
            above = [[X[src, m * layers, c, mid, :] for c in range(nb)] for m in range(members)]
            here = above
            for l in range(layers):
                total = [None] * nb
                after = []
                for m in range(members):
                    p = m * layers + l
                    below = [X[src, p + 1, c, mid, :] for c in range(nb)] if l < layers - 1 else here[m]
                    after.append(below)
                    side = sideways([W[src, p, c, mid, :] for c in range(nb)])
                    for c in range(nb):
                        planar = side[c] + (W[src, p, c, up, :] + W[src, p, c, down, :])
                        new = C[l, c, mid, :] * here[m][c] + planar + VERT * (above[m][c] + below[c])
                        if l == 0 or l == layers - 1:
                            pass
                        if last:
                            adj[m, l, pl.ds(pl.multiple_of(8 * i, 8), 8), cols_of(c)] = new
                        else:
                            X[dst, p, c, mid, :] = new
                            W[dst, p, c, mid, :] = K[l, c, mid, :] * new
                            part = new + here[m][c] if k == 0 else new
                            total[c] = part if total[c] is None else total[c] + part
                if not last:
                    for c in range(nb):
                        RS[i, l, c] = total[c] if k == 0 else RS[i, l, c] + total[c]
                above, here = here, after
            if last:
                row_copy(adj, adj_out, sems, i).start()
            return carry

        lax.fori_loop(0, rows // 8 if last else chunks, chunk, 0, unroll=True)
        if k == ITERS - 2:
            row = lax.broadcasted_iota(jnp.int32, (8, LANES), 0)
            BS[...] = jnp.zeros_like(BS)
            for l in range(layers):
                for c in range(nb):
                    sums = [jnp.zeros((8, LANES), f32)] * 2
                    done = HALO
                    for i in range(chunks):
                        start = min(1 + 8 * i, rows + 2 * HALO - 9)
                        value = RS[i, l, c]
                        for b in range(2):
                            lo = max(done, HALO + R * b) - start
                            hi = min(start + 8, HALO + R * (b + 1)) - start
                            if hi <= max(lo, 0):
                                continue
                            part = value if lo <= 0 and hi >= 8 else jnp.where((row >= lo) & (row < hi), value, 0.0)
                            sums[b] = sums[b] + part
                        done = start + 8
                    for b in range(2):
                        BS[2 * l + b:2 * l + b + 1, cols_of(c)] = jnp.sum(sums[b], axis=0, keepdims=True)
            packed = jnp.zeros((8, LANES), f32)
            for g in range(BS.shape[0] // 8):
                packed = packed + jnp.dot(BS[8 * g:8 * g + 8, :], spread(g, R, cols), precision=HIGHEST)
            packed = packed * (RELAX / (R * R))
            blocks[...] = jnp.zeros_like(blocks)
            spaces = tile_map.shape[0]
            owner = tile_map[position]
            for m in range(blocks.shape[0] // spaces):
                blocks[m * spaces + owner] = packed
            send_blocks.start()
    for i in range(rows // 8):
        row_copy(adj, adj_out, sems, i).wait()
    send_blocks.wait()


def forward_kernel(temp, forcing_in, a_msg, b_msg, soil, cond, tiles, tile_map, result, X, K, C, S, T, F, TE, out, forcing, sems, sem):
    get_temp = pltpu.make_async_copy(temp, out, sem.at[0])
    get_forcing = pltpu.make_async_copy(forcing_in, forcing, sem.at[1])
    get_temp.start()
    get_forcing.start()
    members, layers, rows, cols = temp.shape
    spaces = tile_map.shape[0]
    position = lax.axis_index("space")
    odd = position % 2
    nb = cols // LANES
    ext = rows + 2 * HALO
    fill_kappa(soil, a_msg, b_msg, cond, odd, layers, S, K, C)
    around = []
    for shift in (-1, 0, 1):
        where = jnp.minimum(jnp.maximum(position + shift, 0), spaces - 1)
        inside = jnp.logical_and(position + shift >= 0, position + shift < spaces)
        around.append(jnp.where(inside, tiles[tile_map[where]], 0.0))
    stack = jnp.concatenate(around, axis=0) * RELAX
    for g in range(TE.shape[0]):
        lane = lax.broadcasted_iota(jnp.int32, (LANES, cols), 0)
        y = lax.broadcasted_iota(jnp.int32, (LANES, cols), 1)
        TE[g] = jnp.dot(stack, (y // R + 32 * g == lane).astype(f32), precision=HIGHEST)

    def levels(l, t, b):
        n = 2 * l + b
        return TE[n // 8, 8 * t + n % 8:8 * t + n % 8 + 1, :]

    for l in range(layers):
        bands = [(0, HALO, levels(l, 0, 1)), (HALO, HALO + R, levels(l, 1, 0)), (HALO + R, HALO + 2 * R, levels(l, 1, 1)), (HALO + 2 * R, ext, levels(l, 2, 0))]
        for c in range(nb):
            for lo, hi, value in bands:
                T[l, c, lo:hi, :] = jnp.broadcast_to(value[:, cols_of(c)], (hi - lo, LANES))
    get_temp.wait()
    fill_field(out, a_msg, b_msg, odd, X, members * layers)
    get_forcing.wait()
    for m in range(members):
        top, bottom = side_rows(odd, a_msg, b_msg, 2 * members * layers + m)
        for c in range(nb):
            F[m, c, 0:HALO, :] = T[0, c, 0:HALO, :] + top[:, cols_of(c)]
            F[m, c, rows + HALO:, :] = T[0, c, rows + HALO:, :] + bottom[:, cols_of(c)]
            F[m, c, HALO:rows + HALO, :] = T[0, c, HALO:rows + HALO, :] + forcing[m, :, cols_of(c)]

    for k in range(ITERS):
        src, dst = k % 2, 1 - k % 2
        last = k == ITERS - 1

        def chunk(i, carry):
            r = HALO + 8 * i if last else chunk_start(i, rows)
            mid, up, down = pl.ds(r, 8), pl.ds(r - 1, 8), pl.ds(r + 1, 8)
            above = [[X[src, m * layers, c, mid, :] for c in range(nb)] for m in range(members)]
            here = above
            for l in range(layers):
                after = []
                for m in range(members):
                    p = m * layers + l
                    below = [X[src, p + 1, c, mid, :] for c in range(nb)] if l < layers - 1 else here[m]
                    after.append(below)
                    side = sideways(here[m])
                    for c in range(nb):
                        around = side[c] + (X[src, p, c, up, :] + X[src, p, c, down, :])
                        source = F[m, c, mid, :] if l == 0 else T[l, c, mid, :]
                        new = C[l, c, mid, :] * here[m][c] + K[l, c, mid, :] * around + (VERT * (above[m][c] + below[c]) + source)
                        if last:
                            out[m, l, pl.ds(pl.multiple_of(8 * i, 8), 8), cols_of(c)] = new
                        else:
                            X[dst, p, c, mid, :] = new
                above, here = here, after
            if last:
                row_copy(out, result, sems, i).start()
            return carry

        lax.fori_loop(0, rows // 8 if last else -(-(ext - 2) // 8), chunk, 0, unroll=True)
    for i in range(rows // 8):
        row_copy(out, result, sems, i).wait()


def sum_kernel(received, out, total):
    value = received[0]
    for i in range(1, received.shape[0]):
        value = value + received[i]
    total[...] = value
    layers, per, width = out.shape
    for l in range(layers):
        for b in range(per):
            n = per * l + b
            out[l, b:b + 1, :] = total[n % 8:n % 8 + 1, 32 * (n // 8):32 * (n // 8) + width]


def body(temp_start, cotangent, forcing, soil_class, conductivity, parent_field, tile_map):
    members, layers, rows, cols = temp_start.shape
    nb = cols // LANES
    spaces = lax.axis_size("space")
    groups = lax.axis_size("member")
    planes = members * layers
    ext = rows + 2 * HALO
    chunks = -(-(ext - 2) // 8)
    pieces = -(-2 * layers // 8)
    shape = lambda *dims: jax.ShapeDtypeStruct(dims, f32)
    local = lambda *dims: pltpu.VMEM(dims, f32)
    edges = lambda kind, *dims: pltpu.VMEM((2, *dims, 8, cols), kind)
    total = 2 * planes + members + 1
    a_msg, b_msg, tiles = pl.pallas_call(
        pack_kernel,
        out_shape=(shape(total, HALO, cols), shape(total, HALO, cols), shape(spaces, 8, LANES)),
        in_specs=[HB] * 5,
        out_specs=[VM] * 3,
        scratch_shapes=[
            pltpu.VMEM((8 * pieces, parent_field.shape[2]), f32),
            edges(f32, members, layers),
            edges(f32, members, layers),
            edges(f32, members),
            edges(jnp.int32),
            pltpu.VMEM(parent_field.shape, f32),
            pltpu.SemaphoreType.DMA((4, 2)),
            pltpu.SemaphoreType.DMA,
        ],
        compiler_params=SMALL,
        name="pack",
    )(far(cotangent), far(temp_start), far(forcing), far(soil_class), far(parent_field))
    pair = [(i, i ^ 1) for i in range(spaces)]
    across = [(i, i + 1) for i in range(1, spaces - 1, 2)] + [(i + 1, i) for i in range(1, spaces - 1, 2)]
    a_msg = near(lax.ppermute(a_msg, "space", pair))
    b_msg = near(lax.ppermute(b_msg, "space", across))
    tiles = lax.all_to_all(tiles, "space", 0, 0, tiled=True)
    flops = 15 * planes * ext * cols * ITERS
    cost = pl.CostEstimate(flops=flops, bytes_accessed=4 * 2 * planes * rows * cols, transcendentals=0)
    adjoint, blocks = pl.pallas_call(
        adjoint_kernel,
        out_shape=(
            shape(*cotangent.shape),
            shape(groups * spaces, 8, LANES),
        ),
        in_specs=[VM, VM, VM, VM, SM, SM],
        out_specs=[HB, HB],
        scratch_shapes=[
            pltpu.VMEM((2, planes, nb, ext, LANES), f32),
            pltpu.VMEM((2, planes, nb, ext, LANES), f32),
            pltpu.VMEM((layers, nb, ext, LANES), f32),
            pltpu.VMEM((layers, nb, ext, LANES), f32),
            pltpu.VMEM((nb, ext, LANES), jnp.int32),
            pltpu.VMEM((chunks, layers, nb, 8, LANES), f32),
            pltpu.VMEM((8 * pieces, cols), f32),
            pltpu.VMEM((groups * spaces, 8, LANES), f32),
            pltpu.VMEM(cotangent.shape, f32),
            pltpu.SemaphoreType.DMA((rows // 8,)),
            pltpu.SemaphoreType.DMA((1,)),
        ],
        compiler_params=PARAMS,
        cost_estimate=cost,
        name="adjoint",
    )(near(cotangent), a_msg, b_msg, near(soil_class), conductivity, tile_map)
    blocks, tiles = lax.optimization_barrier((blocks, tiles))
    received = lax.all_to_all(blocks, ("member", "space"), 0, 0, tiled=True)
    final = pl.pallas_call(
        forward_kernel,
        out_shape=shape(*temp_start.shape),
        in_specs=[HB, HB] + [VM] * 3 + [SM, VM, SM],
        out_specs=HB,
        scratch_shapes=[
            pltpu.VMEM((2, planes, nb, ext, LANES), f32),
            pltpu.VMEM((layers, nb, ext, LANES), f32),
            pltpu.VMEM((layers, nb, ext, LANES), f32),
            pltpu.VMEM((nb, ext, LANES), jnp.int32),
            pltpu.VMEM((layers, nb, ext, LANES), f32),
            pltpu.VMEM((members, nb, ext, LANES), f32),
            pltpu.VMEM((pieces, 24, cols), f32),
            pltpu.VMEM(temp_start.shape, f32),
            pltpu.VMEM(forcing.shape, f32),
            pltpu.SemaphoreType.DMA((rows // 8,)),
            pltpu.SemaphoreType.DMA((2,)),
        ],
        compiler_params=PARAMS,
        cost_estimate=cost,
        name="forward",
    )(far(temp_start), far(forcing), a_msg, b_msg, near(soil_class), conductivity, tiles, tile_map)
    parent_grad = pl.pallas_call(
        sum_kernel,
        out_shape=jax.ShapeDtypeStruct(parent_field.shape, f32),
        in_specs=[VM],
        out_specs=VM,
        scratch_shapes=[pltpu.VMEM((8, LANES), f32)],
        compiler_params=PARAMS,
        name="collect",
    )(near(received))
    return final, adjoint, parent_grad


def solution(mesh):
    return jax.shard_map(
        body,
        mesh=mesh,
        in_specs=(
            P("member", None, "space", None),
            P("member", None, "space", None),
            P("member", "space", None),
            P("space", None),
            P(),
            P(None, "space", None),
            P(),
        ),
        out_specs=(
            P("member", None, "space", None),
            P("member", None, "space", None),
            P(None, "space", None),
        ),
        check_vma=False,
    )
```

```python
import functools

import jax
import jax.numpy as jnp
from jax import lax
from jax.experimental import pallas as pl
from jax.experimental.pallas import tpu as pltpu
from jax.sharding import PartitionSpec as P

R = 20
ITERS = 4
HALO = ITERS
LANES = 128
RELAX = 0.1
VERT = 0.05
KEEP = 1.0 - RELAX - 2.0 * VERT
f32 = jnp.float32
HIGHEST = lax.Precision.HIGHEST

VM = pl.BlockSpec(memory_space=pltpu.VMEM)
SM = pl.BlockSpec(memory_space=pltpu.SMEM)
HB = pl.BlockSpec(memory_space=pl.ANY)
SMALL = pltpu.CompilerParams(vmem_limit_bytes=6 * 1024 * 1024)
PARAMS = pltpu.CompilerParams(vmem_limit_bytes=24 * 1024 * 1024)


def far(x):
    return pltpu.with_memory_space_constraint(x, pltpu.HBM)


def near(x):
    return pltpu.with_memory_space_constraint(x, pltpu.VMEM)


def cols_of(c):
    return slice(c * LANES, (c + 1) * LANES)


def spread(group, rows, width):
    y = lax.broadcasted_iota(jnp.int32, (width, LANES), 0)
    lane = lax.broadcasted_iota(jnp.int32, (width, LANES), 1)
    return (y // rows + 32 * group == lane).astype(f32)


def send_rows(odd, pieces):
    for parity in (0, 1):
        @pl.when(odd == parity)
        def _():
            for take, plane, near_msg, far_msg in pieces:
                low, high = take(True), take(False)
                first, second = (far_msg, near_msg) if parity == 0 else (near_msg, far_msg)
                first[plane] = low()
                second[plane] = high()


def taker(ref, *index, convert=None):
    def take(top):
        def get():
            value = ref[(0 if top else 1, *index, slice(0, HALO) if top else slice(8 - HALO, 8), slice(None))]
            return convert(value) if convert else value

        return get

    return take


def edge_copies(pairs, rows, sems):
    out = []
    for n, (field, edges) in enumerate(pairs):
        for side, start in ((0, 0), (1, rows - 8)):
            cut = (*[slice(None)] * (len(field.shape) - 2), pl.ds(start, 8), slice(None))
            out.append(pltpu.make_async_copy(field.at[cut], edges.at[side], sems.at[n, side]))
    return out


def pack_kernel(cot, temp, forcing, soil, parent, a_msg, b_msg, tiles, flat, edge_c, edge_t, edge_f, edge_s, held, sems, sem):
    members, layers, rows = cot.shape[:3]
    get_parent = pltpu.make_async_copy(parent, held, sem)
    get_parent.start()
    copies = edge_copies(((cot, edge_c), (temp, edge_t), (forcing, edge_f), (soil, edge_s)), rows, sems)
    for copy in copies:
        copy.start()
    odd = lax.axis_index("space") % 2
    flat[...] = jnp.zeros_like(flat)
    get_parent.wait()
    for l in range(layers):
        flat[2 * l:2 * l + 2, :] = held[l]
    packed = jnp.zeros((8, LANES), f32)
    for g in range(flat.shape[0] // 8):
        packed = packed + jnp.dot(flat[8 * g:8 * g + 8, :], spread(g, 1, flat.shape[1]), precision=HIGHEST)
    for i in range(tiles.shape[0]):
        tiles[i] = packed
    for copy in copies:
        copy.wait()
    planes = members * layers
    pieces = []
    for m in range(members):
        for l in range(layers):
            pieces.append((taker(edge_c, m, l), m * layers + l, a_msg, b_msg))
            pieces.append((taker(edge_t, m, l), planes + m * layers + l, a_msg, b_msg))
        pieces.append((taker(edge_f, m), 2 * planes + m, a_msg, b_msg))
    pieces.append((taker(edge_s, convert=lambda v: v.astype(f32) + 1.0), 2 * planes + members, a_msg, b_msg))
    send_rows(odd, pieces)


def side_rows(odd, a_ref, b_ref, p):
    a, b = a_ref[p], b_ref[p]
    return jnp.where(odd == 1, a, b), jnp.where(odd == 1, b, a)


def fill_kappa(soil, a_msg, b_msg, cond, odd, layers, S, K, C):
    rows, cols = soil.shape
    top, bottom = side_rows(odd, a_msg, b_msg, a_msg.shape[0] - 1)
    lane = lax.broadcasted_iota(jnp.int32, (8, LANES), 1)
    for c in range(cols // LANES):
        S[c, 0:HALO, :] = top[:, cols_of(c)].astype(jnp.int32) - 1
        S[c, rows + HALO:, :] = bottom[:, cols_of(c)].astype(jnp.int32) - 1
        S[c, HALO:rows + HALO, :] = soil[:, cols_of(c)]
    classes = cond.shape[0]
    for l in range(layers):
        table = jnp.zeros((8, LANES), f32)
        for k in range(classes):
            table = jnp.where(lane == k, cond[k, l], table)
        for c in range(cols // LANES):
            for i in range((rows + 2 * HALO) // 8):
                cut = slice(8 * i, 8 * i + 8)
                idx = S[c, cut, :]
                idx = jnp.where(idx < 0, LANES - 1, idx)
                kappa = jnp.take_along_axis(table, idx, axis=1)
                K[l, c, cut, :] = kappa
                C[l, c, cut, :] = KEEP - 4.0 * kappa


def fill_field(field, a_ref, b_ref, odd, X, first):
    members, layers, rows, cols = field.shape

    def plane(p, carry):
        top, bottom = side_rows(odd, a_ref, b_ref, first + p)
        for c in range(cols // LANES):
            X[0, p, c, 0:HALO, :] = top[:, cols_of(c)]
            X[0, p, c, rows + HALO:, :] = bottom[:, cols_of(c)]
            X[0, p, c, HALO:rows + HALO, :] = field[p // layers, p % layers, :, cols_of(c)]
        return carry

    lax.fori_loop(0, members * layers, plane, 0)


def sideways(center):
    lane = lax.broadcasted_iota(jnp.int32, (8, LANES), 1)
    count = len(center)
    right = [pltpu.roll(v, 1, 1) for v in center]
    left = [pltpu.roll(v, LANES - 1, 1) for v in center]
    out = []
    for c in range(count):
        before = right[c - 1] if c > 0 else jnp.zeros((8, LANES), f32)
        after = left[c + 1] if c < count - 1 else jnp.zeros((8, LANES), f32)
        out.append(jnp.where(lane == 0, before, right[c]) + jnp.where(lane == LANES - 1, after, left[c]))
    return out


def chunk_start(i, rows):
    return jnp.minimum(1 + 8 * i, rows + 2 * HALO - 9)


def row_copy(src, dst, sems, i):
    cut = pl.ds(pl.multiple_of(8 * i, 8), 8)
    return pltpu.make_async_copy(src.at[:, :, cut, :], dst.at[:, :, cut, :], sems.at[i])


def adjoint_kernel(cot, a_msg, b_msg, soil, cond, tile_map, adj_out, blocks_out, X, W, K, C, S, RS, BS, blocks, adj, sems, sem):
    members, layers, rows, cols = cot.shape
    position = lax.axis_index("space")
    odd = position % 2
    nb = cols // LANES
    chunks = RS.shape[0]
    send_blocks = pltpu.make_async_copy(blocks, blocks_out, sem.at[0])
    fill_kappa(soil, a_msg, b_msg, cond, odd, layers, S, K, C)
    fill_field(cot, a_msg, b_msg, odd, X, 0)

    def weigh(p, carry):
        for c in range(nb):
            W[0, p, c] = X[0, p, c] * K[p % layers, c]
        return carry

    lax.fori_loop(0, members * layers, weigh, 0)

    for k in range(ITERS):
        src, dst = k % 2, 1 - k % 2
        last = k == ITERS - 1

        def chunk(i, carry):
            r = HALO + 8 * i if last else chunk_start(i, rows)
            mid, up, down = pl.ds(r, 8), pl.ds(r - 1, 8), pl.ds(r + 1, 8)
            above = [[X[src, m * layers, c, mid, :] for c in range(nb)] for m in range(members)]
            here = above
            for l in range(layers):
                total = [None] * nb
                after = []
                for m in range(members):
                    p = m * layers + l
                    below = [X[src, p + 1, c, mid, :] for c in range(nb)] if l < layers - 1 else here[m]
                    after.append(below)
                    side = sideways([W[src, p, c, mid, :] for c in range(nb)])
                    for c in range(nb):
                        planar = side[c] + (W[src, p, c, up, :] + W[src, p, c, down, :])
                        new = C[l, c, mid, :] * here[m][c] + planar + VERT * (above[m][c] + below[c])
                        if l == 0 or l == layers - 1:
                            pass
                        if last:
                            adj[m, l, pl.ds(pl.multiple_of(8 * i, 8), 8), cols_of(c)] = new
                        else:
                            X[dst, p, c, mid, :] = new
                            W[dst, p, c, mid, :] = K[l, c, mid, :] * new
                            part = new + here[m][c] if k == 0 else new
                            total[c] = part if total[c] is None else total[c] + part
                if not last:
                    for c in range(nb):
                        RS[i, l, c] = total[c] if k == 0 else RS[i, l, c] + total[c]
                above, here = here, after
            if last:
                row_copy(adj, adj_out, sems, i).start()
            return carry

        lax.fori_loop(0, rows // 8 if last else chunks, chunk, 0, unroll=True)
        if k == ITERS - 2:
            row = lax.broadcasted_iota(jnp.int32, (8, LANES), 0)
            BS[...] = jnp.zeros_like(BS)
            for l in range(layers):
                for c in range(nb):
                    sums = [jnp.zeros((8, LANES), f32)] * 2
                    done = HALO
                    for i in range(chunks):
                        start = min(1 + 8 * i, rows + 2 * HALO - 9)
                        value = RS[i, l, c]
                        for b in range(2):
                            lo = max(done, HALO + R * b) - start
                            hi = min(start + 8, HALO + R * (b + 1)) - start
                            if hi <= max(lo, 0):
                                continue
                            part = value if lo <= 0 and hi >= 8 else jnp.where((row >= lo) & (row < hi), value, 0.0)
                            sums[b] = sums[b] + part
                        done = start + 8
                    for b in range(2):
                        BS[2 * l + b:2 * l + b + 1, cols_of(c)] = jnp.sum(sums[b], axis=0, keepdims=True)
            packed = jnp.zeros((8, LANES), f32)
            for g in range(BS.shape[0] // 8):
                packed = packed + jnp.dot(BS[8 * g:8 * g + 8, :], spread(g, R, cols), precision=HIGHEST)
            packed = packed * (RELAX / (R * R))
            blocks[...] = jnp.zeros_like(blocks)
            spaces = tile_map.shape[0]
            owner = tile_map[position]
            for m in range(blocks.shape[0] // spaces):
                blocks[m * spaces + owner] = packed
            send_blocks.start()
    for i in range(rows // 8):
        row_copy(adj, adj_out, sems, i).wait()
    send_blocks.wait()


def forward_kernel(temp, forcing_in, a_msg, b_msg, soil, cond, tiles, tile_map, result, X, K, C, S, T, F, TE, out, forcing, sems, sem):
    get_temp = pltpu.make_async_copy(temp, out, sem.at[0])
    get_forcing = pltpu.make_async_copy(forcing_in, forcing, sem.at[1])
    get_temp.start()
    get_forcing.start()
    members, layers, rows, cols = temp.shape
    spaces = tile_map.shape[0]
    position = lax.axis_index("space")
    odd = position % 2
    nb = cols // LANES
    ext = rows + 2 * HALO
    fill_kappa(soil, a_msg, b_msg, cond, odd, layers, S, K, C)
    around = []
    for shift in (-1, 0, 1):
        where = jnp.minimum(jnp.maximum(position + shift, 0), spaces - 1)
        inside = jnp.logical_and(position + shift >= 0, position + shift < spaces)
        around.append(jnp.where(inside, tiles[tile_map[where]], 0.0))
    stack = jnp.concatenate(around, axis=0) * RELAX
    for g in range(TE.shape[0]):
        lane = lax.broadcasted_iota(jnp.int32, (LANES, cols), 0)
        y = lax.broadcasted_iota(jnp.int32, (LANES, cols), 1)
        TE[g] = jnp.dot(stack, (y // R + 32 * g == lane).astype(f32), precision=HIGHEST)

    def levels(l, t, b):
        n = 2 * l + b
        return TE[n // 8, 8 * t + n % 8:8 * t + n % 8 + 1, :]

    for l in range(layers):
        bands = [(0, HALO, levels(l, 0, 1)), (HALO, HALO + R, levels(l, 1, 0)), (HALO + R, HALO + 2 * R, levels(l, 1, 1)), (HALO + 2 * R, ext, levels(l, 2, 0))]
        for c in range(nb):
            for lo, hi, value in bands:
                T[l, c, lo:hi, :] = jnp.broadcast_to(value[:, cols_of(c)], (hi - lo, LANES))
    get_temp.wait()
    fill_field(out, a_msg, b_msg, odd, X, members * layers)
    get_forcing.wait()
    for m in range(members):
        top, bottom = side_rows(odd, a_msg, b_msg, 2 * members * layers + m)
        for c in range(nb):
            F[m, c, 0:HALO, :] = T[0, c, 0:HALO, :] + top[:, cols_of(c)]
            F[m, c, rows + HALO:, :] = T[0, c, rows + HALO:, :] + bottom[:, cols_of(c)]
            F[m, c, HALO:rows + HALO, :] = T[0, c, HALO:rows + HALO, :] + forcing[m, :, cols_of(c)]

    for k in range(ITERS):
        src, dst = k % 2, 1 - k % 2
        last = k == ITERS - 1

        def chunk(i, carry):
            r = HALO + 8 * i if last else chunk_start(i, rows)
            mid, up, down = pl.ds(r, 8), pl.ds(r - 1, 8), pl.ds(r + 1, 8)
            above = [[X[src, m * layers, c, mid, :] for c in range(nb)] for m in range(members)]
            here = above
            for l in range(layers):
                after = []
                for m in range(members):
                    p = m * layers + l
                    below = [X[src, p + 1, c, mid, :] for c in range(nb)] if l < layers - 1 else here[m]
                    after.append(below)
                    side = sideways(here[m])
                    for c in range(nb):
                        around = side[c] + (X[src, p, c, up, :] + X[src, p, c, down, :])
                        source = F[m, c, mid, :] if l == 0 else T[l, c, mid, :]
                        new = C[l, c, mid, :] * here[m][c] + K[l, c, mid, :] * around + (VERT * (above[m][c] + below[c]) + source)
                        if last:
                            out[m, l, pl.ds(pl.multiple_of(8 * i, 8), 8), cols_of(c)] = new
                        else:
                            X[dst, p, c, mid, :] = new
                above, here = here, after
            if last:
                row_copy(out, result, sems, i).start()
            return carry

        lax.fori_loop(0, rows // 8 if last else -(-(ext - 2) // 8), chunk, 0, unroll=True)
    for i in range(rows // 8):
        row_copy(out, result, sems, i).wait()


def sum_kernel(received, out, total):
    value = received[0]
    for i in range(1, received.shape[0]):
        value = value + received[i]
    total[...] = value
    layers, per, width = out.shape
    for l in range(layers):
        for b in range(per):
            n = per * l + b
            out[l, b:b + 1, :] = total[n % 8:n % 8 + 1, 32 * (n // 8):32 * (n // 8) + width]


def body(temp_start, cotangent, forcing, soil_class, conductivity, parent_field, tile_map):
    members, layers, rows, cols = temp_start.shape
    nb = cols // LANES
    spaces = lax.axis_size("space")
    groups = lax.axis_size("member")
    planes = members * layers
    ext = rows + 2 * HALO
    chunks = -(-(ext - 2) // 8)
    pieces = -(-2 * layers // 8)
    shape = lambda *dims: jax.ShapeDtypeStruct(dims, f32)
    local = lambda *dims: pltpu.VMEM(dims, f32)
    edges = lambda kind, *dims: pltpu.VMEM((2, *dims, 8, cols), kind)
    total = 2 * planes + members + 1
    a_msg, b_msg, tiles = pl.pallas_call(
        pack_kernel,
        out_shape=(shape(total, HALO, cols), shape(total, HALO, cols), shape(spaces, 8, LANES)),
        in_specs=[HB] * 5,
        out_specs=[VM] * 3,
        scratch_shapes=[
            pltpu.VMEM((8 * pieces, parent_field.shape[2]), f32),
            edges(f32, members, layers),
            edges(f32, members, layers),
            edges(f32, members),
            edges(jnp.int32),
            pltpu.VMEM(parent_field.shape, f32),
            pltpu.SemaphoreType.DMA((4, 2)),
            pltpu.SemaphoreType.DMA,
        ],
        compiler_params=SMALL,
        name="pack",
    )(far(cotangent), far(temp_start), far(forcing), far(soil_class), far(parent_field))
    pair = [(i, i ^ 1) for i in range(spaces)]
    across = [(i, i + 1) for i in range(1, spaces - 1, 2)] + [(i + 1, i) for i in range(1, spaces - 1, 2)]
    a_msg = near(lax.ppermute(a_msg, "space", pair))
    b_msg = near(lax.ppermute(b_msg, "space", across))
    tiles = lax.all_to_all(tiles, "space", 0, 0, tiled=True)
    flops = 15 * planes * ext * cols * ITERS
    cost = pl.CostEstimate(flops=flops, bytes_accessed=4 * 2 * planes * rows * cols, transcendentals=0)
    adjoint, blocks = pl.pallas_call(
        adjoint_kernel,
        out_shape=(
            shape(*cotangent.shape),
            pltpu.HBM((groups * spaces, 8, LANES), f32),
        ),
        in_specs=[VM, VM, VM, VM, SM, SM],
        out_specs=[HB, HB],
        scratch_shapes=[
            pltpu.VMEM((2, planes, nb, ext, LANES), f32),
            pltpu.VMEM((2, planes, nb, ext, LANES), f32),
            pltpu.VMEM((layers, nb, ext, LANES), f32),
            pltpu.VMEM((layers, nb, ext, LANES), f32),
            pltpu.VMEM((nb, ext, LANES), jnp.int32),
            pltpu.VMEM((chunks, layers, nb, 8, LANES), f32),
            pltpu.VMEM((8 * pieces, cols), f32),
            pltpu.VMEM((groups * spaces, 8, LANES), f32),
            pltpu.VMEM(cotangent.shape, f32),
            pltpu.SemaphoreType.DMA((rows // 8,)),
            pltpu.SemaphoreType.DMA((1,)),
        ],
        compiler_params=PARAMS,
        cost_estimate=cost,
        name="adjoint",
    )(near(cotangent), a_msg, b_msg, near(soil_class), conductivity, tile_map)
    blocks, tiles = lax.optimization_barrier((blocks, tiles))
    received = lax.all_to_all(blocks, ("member", "space"), 0, 0, tiled=True)
    final = pl.pallas_call(
        forward_kernel,
        out_shape=shape(*temp_start.shape),
        in_specs=[HB, HB] + [VM] * 3 + [SM, VM, SM],
        out_specs=HB,
        scratch_shapes=[
            pltpu.VMEM((2, planes, nb, ext, LANES), f32),
            pltpu.VMEM((layers, nb, ext, LANES), f32),
            pltpu.VMEM((layers, nb, ext, LANES), f32),
            pltpu.VMEM((nb, ext, LANES), jnp.int32),
            pltpu.VMEM((layers, nb, ext, LANES), f32),
            pltpu.VMEM((members, nb, ext, LANES), f32),
            pltpu.VMEM((pieces, 24, cols), f32),
            pltpu.VMEM(temp_start.shape, f32),
            pltpu.VMEM(forcing.shape, f32),
            pltpu.SemaphoreType.DMA((rows // 8,)),
            pltpu.SemaphoreType.DMA((2,)),
        ],
        compiler_params=PARAMS,
        cost_estimate=cost,
        name="forward",
    )(far(temp_start), far(forcing), a_msg, b_msg, near(soil_class), conductivity, tiles, tile_map)
    parent_grad = pl.pallas_call(
        sum_kernel,
        out_shape=jax.ShapeDtypeStruct(parent_field.shape, f32),
        in_specs=[VM],
        out_specs=VM,
        scratch_shapes=[pltpu.VMEM((8, LANES), f32)],
        compiler_params=PARAMS,
        name="collect",
    )(near(received))
    return final, adjoint, parent_grad


def solution(mesh):
    return jax.shard_map(
        body,
        mesh=mesh,
        in_specs=(
            P("member", None, "space", None),
            P("member", None, "space", None),
            P("member", "space", None),
            P("space", None),
            P(),
            P(None, "space", None),
            P(),
        ),
        out_specs=(
            P("member", None, "space", None),
            P("member", None, "space", None),
            P(None, "space", None),
        ),
        check_vma=False,
    )
```
